32 devices in a mesh: ens: 2 (over x), tm: 16 (over z, y, core).
Axes of the slice: x: 2, y: 2, z: 4, core: 2. Of those that a mesh axis runs over, the one named last changes fastest.
Arguments:
- observed: float32 [32, 3000], P(('ens', 'tm')), parts along dimension 0, may hold values from -6 to 6
- present: int32 [32, 3000], P(('ens', 'tm')), parts along dimension 0, may hold values 0 or 1
- loading: float32 [3000, 16], replicated, may hold values from -1.5 to 1.5
- noise_var: float32 [3000], replicated, may hold values from 0.25 to 1
- region_block: int32 [3000], replicated, may hold values from 0 to 127
- transition: float32 [16, 16, 128], replicated, may hold values from -1 to 1
- innovation: float32 [2048], replicated, may hold values from 0.05 to 0.5
- prior_mean: float32 [2048], replicated, may hold values from -4 to 4
- prior_var: float32 [2048], replicated, may hold values from 0.5 to 2
Outputs:
- filtered_mean: float32 [32, 2048], P(('ens', 'tm')), parts along dimension 0
- smoothed_mean: float32 [32, 2048], P(('ens', 'tm')), parts along dimension 0
- smoothed_var: float32 [32, 2048], P(('ens', 'tm')), parts along dimension 0
The draws below stay inside these ranges and needn't reach their ends.
There are 2 independent parts, one for each index of `ens`. The reference program is written for one: setup_inputs(seed, part) draws one part's arguments, and reference() takes and returns one part's arrays. A program takes and returns all parts, laid end to end along the dimension named above; an argument that names none is the same for every part. Nothing has to cross between parts.
All inputs are finite; a program needn't handle non-finite values. No bound on the sum of `present` on one device may be relied on, other than what follows from the above.
Results may differ from the reference program's by a relative error of at most 0.0003.
Values sent between devices are 32-bit elements; how exact they have to be, the bound alone decides.
A program may use at most 128 MiB of HBM per device.

```python
import math
import jax
import jax.numpy as jnp
from jax import lax

FACTORS = 2048
BLOCK = 16
NBLOCKS = 128
REGIONS = 3000
HOURS = 16


def draw_transition(key, part):
    rate_key = jax.random.fold_in(key, 11)
    turn_key = jax.random.fold_in(key, 23)
    spread = jax.random.uniform(rate_key, (BLOCK, NBLOCKS), jnp.float32)
    lowest = jnp.log(0.25 / HOURS)
    highest = jnp.log(1.0 / 30.0)
    rate = jnp.exp(lowest + spread * (highest - lowest))
    keeping = jnp.exp(-rate)
    direction = jax.random.normal(turn_key, (BLOCK, NBLOCKS), jnp.float32)
    length_sq = jnp.sum(direction * direction, axis=0)
    reflect = jnp.eye(BLOCK, dtype=jnp.float32)[:, :, None] - 2.0 * direction[:, None, :] * direction[None, :, :] / length_sq[None, None, :]
    rooted = jnp.sqrt(keeping)
    return rooted[:, None, :] * reflect * rooted[None, :, :]


def touch_ends(drawn, key, low, largest):
    shape = drawn.shape
    spot = [jax.random.randint(jax.random.fold_in(key, axis), (), 0, shape[axis]) for axis in range(len(shape))]
    drawn = drawn.at[tuple(spot)].set(low)
    longest = shape.index(max(shape))
    spot[longest] = (spot[longest] + 1) % shape[longest]
    return drawn.at[tuple(spot)].set(largest)


def levels(own_key, extent, shards, low, top_value):
    def one(axis_at, shards_of):
        steps = jax.random.uniform(jax.random.fold_in(jax.random.fold_in(own_key, 6), axis_at), (shards_of,), jnp.float32, low / len(shards), top_value / len(shards))
        return jnp.repeat(jnp.exp(steps), extent[axis_at] // shards_of).reshape((-1,) + (1,) * (len(extent) - axis_at - 1))

    level = one(*shards[0])
    for cut in shards[1:]:
        level = level * one(*cut)
    return level


def bell_draw(rng, shape, scale, most, cuts=(), kind=jnp.bfloat16):
    gain = levels(rng, shape, cuts, -0.22, 0.18) if cuts else 1.0
    result = jax.random.normal(rng, shape, jnp.float32) * scale * gain
    return jnp.minimum(jnp.maximum(result, -most), most).astype(kind)


def setup_inputs(seed: int = 0, part: int = 0) -> dict:
    key_list = jax.random.split(jax.random.key(seed), 10)
    part_splits = jax.random.split(jax.random.fold_in(key_list[9], part), 10)
    observed = bell_draw(part_splits[0], (HOURS, REGIONS), 1.0, 6.0, ((0, 16),), jnp.float32)
    present = touch_ends((jax.random.randint(part_splits[1], (HOURS, REGIONS), 0, 2) < 1).astype(jnp.int32), jax.random.fold_in(part_splits[1], 1), 0, 1)
    loading = bell_draw(key_list[2], (REGIONS, BLOCK), 0.25, 1.5, (), jnp.float32)
    noise_var = jnp.clip(jnp.exp(jax.random.uniform(key_list[3], (REGIONS,), jnp.float32, math.log(0.25), math.log(1.0))), 0.25, 1.0)
    region_block = touch_ends(jax.random.randint(key_list[4], (REGIONS,), 0, NBLOCKS), jax.random.fold_in(key_list[4], 1), 0, NBLOCKS - 1).astype(jnp.int32)
    transition = draw_transition(jax.random.fold_in(key_list[9], 71), part)
    innovation = jnp.clip(jnp.exp(jax.random.uniform(key_list[6], (FACTORS,), jnp.float32, math.log(0.05), math.log(0.5))), 0.05, 0.5)
    prior_mean = bell_draw(key_list[7], (FACTORS,), 1.0, 4.0, (), jnp.float32)
    prior_var = jnp.clip(jnp.exp(jax.random.uniform(key_list[8], (FACTORS,), jnp.float32, math.log(0.5), math.log(2.0))), 0.5, 2.0)
    return {"observed": observed, "present": present, "loading": loading, "noise_var": noise_var, "region_block": region_block, "transition": transition, "innovation": innovation, "prior_mean": prior_mean, "prior_var": prior_var}


exactness = lax.Precision.HIGHEST

def information(observed, present, loading, noise_var, region_block, blocks):
    hours_all, regions_all = observed.shape
    width = loading.shape[1]
    span = regions_all // 12
    weight = present.astype(jnp.float32) / noise_var[None, :]
    weight_parts = jnp.transpose(weight.reshape(hours_all, 12, span), (1, 0, 2))
    value_parts = jnp.transpose((weight * observed).reshape(hours_all, 12, span), (1, 0, 2))
    load_parts = loading.reshape(12, span, width)
    index_parts = region_block.reshape(12, span)

    def accumulate(carried, portion):
        weight_now, value_now, load_now, index_now = portion
        onehot = (index_now[:, None] == lax.iota(jnp.int32, blocks)[None, :]).astype(jnp.float32)
        paired = (load_now[:, :, None] * load_now[:, None, :]).reshape(span, width * width)
        scaled = weight_now[:, :, None] * paired[None, :, :]
        obs_part = jnp.einsum('trk,rb->tkb', scaled, onehot, precision=exactness)
        vec_part = jnp.einsum('tri,rb->tib', value_now[:, :, None] * load_now[None, :, :], onehot, precision=exactness)
        return ((carried[0] + obs_part, carried[1] + vec_part), None)
    start = (jnp.zeros((hours_all, width * width, blocks), jnp.float32), jnp.zeros((hours_all, width, blocks), jnp.float32))
    totals, unused = lax.scan(accumulate, start, (weight_parts, value_parts, load_parts, index_parts))
    return (totals[0].reshape(hours_all, width, width, blocks), totals[1])

def product(first_mat, second_mat):
    return jnp.matmul(first_mat, second_mat, precision=exactness)

def swapped(matrix):
    return jnp.swapaxes(matrix, -1, -2)

def reference(observed, present, loading, noise_var, region_block, transition, innovation, prior_mean, prior_var):
    info_obs, info_vec = information(observed, present, loading, noise_var, region_block, NBLOCKS)
    obs_first = jnp.transpose(info_obs, (0, 3, 1, 2))
    vec_first = jnp.transpose(info_vec, (0, 2, 1))
    moving = jnp.transpose(transition, (2, 0, 1))
    identity_mat = jnp.eye(BLOCK, dtype=jnp.float32)

    def on_grid(values):
        return values.reshape(BLOCK, NBLOCKS).T
    noise_mat = identity_mat[None, :, :] * on_grid(innovation)[:, None, :]
    start_cov = identity_mat[None, :, :] * on_grid(prior_var)[:, None, :]

    def forward(carried, inputs):
        mean_pred, cov_pred = carried
        obs_now, vec_now = inputs
        system = identity_mat[None, :, :] + product(cov_pred, obs_now)
        cov_filt = jnp.linalg.solve(system, cov_pred)
        target = mean_pred + product(cov_pred, vec_now[..., None])[..., 0]
        mean_filt = jnp.linalg.solve(system, target[..., None])[..., 0]
        next_mean = product(moving, mean_filt[..., None])[..., 0]
        next_cov = product(product(moving, cov_filt), swapped(moving)) + noise_mat
        return ((next_mean, next_cov), (mean_filt, cov_filt))
    finished, (filt_mean, filt_cov) = lax.scan(forward, (on_grid(prior_mean), start_cov), (obs_first, vec_first))

    def backward(carried, inputs):
        next_mean, next_cov = carried
        mean_now, cov_now = inputs
        predicted = product(product(moving, cov_now), swapped(moving)) + noise_mat
        gain_now = swapped(jnp.linalg.solve(swapped(predicted), product(moving, swapped(cov_now))))
        ahead = next_mean - product(moving, mean_now[..., None])[..., 0]
        smooth_mean = mean_now + product(gain_now, ahead[..., None])[..., 0]
        smooth_cov = cov_now + product(product(gain_now, next_cov - predicted), swapped(gain_now))
        return ((smooth_mean, smooth_cov), (smooth_mean, jnp.diagonal(smooth_cov, axis1=1, axis2=2)))
    carried, (early_mean, early_var) = lax.scan(backward, (filt_mean[-1], filt_cov[-1]), (filt_mean[:-1], filt_cov[:-1]), reverse=True)
    smooth_mean = jnp.concatenate([early_mean, filt_mean[-1:]], axis=0)
    smooth_var = jnp.concatenate([early_var, jnp.diagonal(filt_cov[-1:], axis1=2, axis2=3)], axis=0)

    def to_factors(values):
        return jnp.transpose(values, (0, 2, 1)).reshape(values.shape[0], FACTORS)
    return (to_factors(filt_mean), to_factors(smooth_mean), to_factors(smooth_var))
```

```python
import functools
import jax
import jax.numpy as jnp
from jax import lax
from jax.experimental import pallas as pl
from jax.experimental.pallas import tpu as pltpu
from jax.sharding import PartitionSpec as P

MESH = pl.DeviceIdType.MESH
W = 16
W2 = W * W
LANES = 128
CHUNK = 512


def negative_inverse(rows):
    sub = lax.broadcasted_iota(jnp.int32, (W, LANES), 0)
    rows = list(rows)
    for p in range(W):
        row = rows[p]
        d = 1.0 / row[p : p + 1, :]
        here = sub == p
        scaled = jnp.where(here, -d, row * d)
        for i in range(W):
            if i == p:
                rows[i] = scaled
            else:
                rows[i] = jnp.where(here, 0.0, rows[i]) - row[i : i + 1, :] * scaled
    return rows


def store_rows(ref, rows):
    for i in range(W):
        ref[i * W : (i + 1) * W, :] = rows[i]


def load_rows(ref):
    return [ref[i * W : (i + 1) * W, :] for i in range(W)]


def load_columns(ref):
    return [ref[pl.ds(k, W, stride=W), :] for k in range(W)]


def multiply(out_ref, left_ref, right_rows, turned=False, start=None, mask=None):
    def one(i, carry):
        at = pl.multiple_of(i * W, W)
        total = None
        for k in range(W):
            row = k * W + i if turned else i * W + k
            term = left_ref[pl.ds(row, 1), :] * right_rows[k]
            total = term if total is None else total + term
        if start is not None:
            total = total + start[pl.ds(at, W), :]
        if mask is not None:
            total = jnp.where(mask, total, 0.0)
        out_ref[pl.ds(at, W), :] = total
        return carry

    lax.fori_loop(0, W, one, 0, unroll=4)


def weigh(rows, vector):
    total = rows[0] * vector[0:1, :]
    for k in range(1, W):
        total = total + rows[k] * vector[k : k + 1, :]
    return total


def kernel(
    T,
    obs_ref,
    pres_ref,
    load_ref,
    nv_ref,
    rb_ref,
    trans_ref,
    innov_ref,
    pmean_ref,
    pvar_ref,
    fm_ref,
    sm_ref,
    sv_ref,
    acc,
    stage,
    recv,
    stage2,
    recv2,
    jm,
    km,
    ym,
    bm,
    nm,
    gm,
    em,
    j1,
    k1,
    const,
    info,
    send_sem,
    recv_sem,
    send_sem2,
    recv_sem2,
):
    per = LANES // T
    me = lax.axis_index("tm")
    barrier = pltpu.get_barrier_semaphore()

    def greet(k, c):
        pl.semaphore_signal(
            barrier, inc=1, device_id={"tm": lax.rem(me + k, T)}, device_id_type=MESH
        )
        return c

    lax.fori_loop(1, T, greet, 0)

    total = obs_ref.shape[1]
    row_at = lax.broadcasted_iota(jnp.int32, (LANES, CHUNK), 0)
    block_of = (row_at % T) * per + row_at // T

    def portion(step, c):
        at = pl.ds(pl.multiple_of(step * CHUNK, CHUNK), CHUNK)
        weight = pres_ref[:, at].astype(jnp.float32) / nv_ref[:, at]
        load = load_ref[:, at]
        lw = load * weight
        parts = [lw * load]
        for d in range(1, W // 2 + 1):
            parts.append(lw * pltpu.roll(load, W - d, 0))
        parts.append(lw * obs_ref[:, at])
        high = [p.astype(jnp.bfloat16) for p in parts]
        low = [(p - h.astype(jnp.float32)).astype(jnp.bfloat16) for p, h in zip(parts, high)]
        fill = [jnp.zeros((2 * LANES - W * len(parts), CHUNK), jnp.bfloat16)]
        onehot = (rb_ref[:, at] == block_of).astype(jnp.float32).astype(jnp.bfloat16)
        dims = (((1,), (1,)), ((), ()))
        got = lax.dot_general(
            onehot,
            jnp.concatenate(high + fill, axis=0),
            dims,
            preferred_element_type=jnp.float32,
        ) + lax.dot_general(
            onehot,
            jnp.concatenate(low + fill, axis=0),
            dims,
            preferred_element_type=jnp.float32,
        )

        @pl.when(step == 0)
        def _():
            acc[...] = got

        @pl.when(step > 0)
        def _():
            acc[...] += got

        return c

    lax.fori_loop(0, total // CHUNK, portion, 0)
    if per < 8:
        stage[...] = jnp.zeros_like(stage)
        stage2[...] = jnp.zeros_like(stage2)
    for h in range(2):
        for b in range(per):
            stage[h, pl.ds(b, T, stride=8), :] = acc[
                b * T : (b + 1) * T, h * LANES : (h + 1) * LANES
            ]

    pl.semaphore_wait(barrier, T - 1)

    def first(k):
        peer = lax.rem(me + k, T)
        return pltpu.make_async_remote_copy(
            src_ref=stage.at[:, pl.ds(pl.multiple_of(peer * 8, 8), 8), :],
            dst_ref=recv.at[:, pl.ds(pl.multiple_of(me * 8, 8), 8), :],
            send_sem=send_sem.at[k],
            recv_sem=recv_sem.at[k],
            device_id={"tm": peer},
            device_id_type=MESH,
        )

    def second(k):
        peer = lax.rem(me + k, T)
        return pltpu.make_async_remote_copy(
            src_ref=stage2.at[pl.ds(pl.multiple_of(peer * 8, 8), 8), :],
            dst_ref=recv2.at[pl.ds(pl.multiple_of(me * 8, 8), 8), :],
            send_sem=send_sem2.at[k],
            recv_sem=recv_sem2.at[k],
            device_id={"tm": peer},
            device_id_type=MESH,
        )

    def begin(make):
        def one(k, c):
            make(k).start()
            return c

        lax.fori_loop(1, T, one, 0)

    def finish(make):
        def one(k, c):
            make(k).wait()
            return c

        lax.fori_loop(1, T, one, 0)

    begin(first)
    mine = pl.ds(pl.multiple_of(me * 8, 8), 8)
    recv[:, mine, :] = stage[:, mine, :]

    lane_from = lax.broadcasted_iota(jnp.int32, (LANES, LANES), 0)
    lane_to = lax.broadcasted_iota(jnp.int32, (LANES, LANES), 1)
    pick = (lane_from == me * per + lane_to // T).astype(jnp.float32)
    whole = jnp.concatenate(
        [trans_ref[...], innov_ref[...], pmean_ref[...], pvar_ref[...]], axis=0
    )
    const[...] = jnp.dot(
        whole, pick, precision=lax.Precision.HIGHEST, preferred_element_type=jnp.float32
    )
    sub = lax.broadcasted_iota(jnp.int32, (W, LANES), 0)
    hour = lax.broadcasted_iota(jnp.int32, (W, LANES), 1) % T
    opening = hour == 0
    inv_noise = 1.0 / const[W2 : W2 + W, :]
    inv_prior = 1.0 / const[W2 + 2 * W : W2 + 3 * W, :]
    start_mean = const[W2 + W : W2 + 2 * W, :] * inv_prior
    for i in range(W):
        km[i * W : (i + 1) * W, :] = jnp.where(
            opening, 0.0, -const[i * W : (i + 1) * W, :] * inv_noise[i : i + 1, :]
        )
    flipped = [-r for r in load_rows(km)]
    multiply(jm, const, flipped, turned=True)
    bm[...] = jnp.zeros_like(bm)

    finish(first)
    for h in range(2):
        joined = jnp.concatenate(
            [recv[h, pl.ds(b, T, stride=8), :] for b in range(per)], axis=0
        )
        info[h * LANES : (h + 1) * LANES, :] = joined.T
    diag = jnp.where(opening, inv_prior, inv_noise)
    for i in range(W):
        for j in range(W):
            gap = (j - i) % W
            row = gap * W + i if gap <= W // 2 else (W - gap) * W + j
            ym[i * W + j : i * W + j + 1, :] = info[row : row + 1, :]
    for i in range(W):
        ym[i * W : (i + 1) * W, :] += jnp.where(sub == i, diag, 0.0)
    npair = (W // 2 + 1) * W
    yv = info[npair : npair + W, :] + jnp.where(opening, start_mean, 0.0)
    ev = jnp.zeros((W, LANES), jnp.float32)
    bv = jnp.zeros((W, LANES), jnp.float32)

    rounds = (T - 1).bit_length()

    def doubling(step, carry):
        yv, ev, bv = carry
        s = jnp.left_shift(1, step)
        keep = hour + s <= T - 1
        rows = negative_inverse(
            [ym[i * W : (i + 1) * W, :] + bm[i * W : (i + 1) * W, :] for i in range(W)]
        )
        store_rows(nm, rows)
        drive = weigh(rows, yv + bv)
        krows = load_rows(km)
        xv = ev + weigh(krows, drive)
        multiply(gm, nm, krows)
        multiply(em, km, load_rows(gm), turned=True, start=jm)
        for i in range(W):
            at = slice(i * W, (i + 1) * W)
            bm[at, :] = jnp.where(keep, pltpu.roll(em[at, :], LANES - s, 1), bm[at, :])
        bv = jnp.where(keep, pltpu.roll(xv, LANES - s, 1), bv)
        inside = hour >= s
        for i in range(W):
            at = slice(i * W, (i + 1) * W)
            k1[at, :] = pltpu.roll(km[at, :], s, 1)
            j1[at, :] = pltpu.roll(jm[at, :], s, 1)
        rows = negative_inverse(
            [
                pltpu.roll(ym[i * W : (i + 1) * W, :], s, 1) + jm[i * W : (i + 1) * W, :]
                for i in range(W)
            ]
        )
        store_rows(nm, rows)
        drive = weigh(rows, pltpu.roll(yv, s, 1) + ev)
        columns = load_columns(km)
        yv = yv + weigh(columns, drive)
        multiply(em, nm, columns)
        multiply(ym, km, load_rows(em), start=ym)
        k1rows = load_rows(k1)
        ev = jnp.where(inside, pltpu.roll(ev, s, 1) + weigh(k1rows, drive), 0.0)
        multiply(gm, nm, k1rows)
        grows = load_rows(gm)
        multiply(jm, k1, grows, turned=True, start=j1, mask=inside)
        multiply(em, km, grows)
        km[...] = em[...]
        return yv, ev, bv

    yv, ev, bv = lax.fori_loop(0, rounds, doubling, (yv, ev, bv))

    rows = negative_inverse(load_rows(ym))
    em[0:W, :] = -weigh(rows, yv)
    rows = negative_inverse(
        [ym[i * W : (i + 1) * W, :] + bm[i * W : (i + 1) * W, :] for i in range(W)]
    )
    em[W : 2 * W, :] = -weigh(rows, yv + bv)
    spread = jnp.where(sub == 0, rows[0], 0.0)
    for i in range(1, W):
        spread = spread + jnp.where(sub == i, rows[i], 0.0)
    em[2 * W : 3 * W, :] = -spread
    em[3 * W : 8 * W, :] = jnp.zeros((5 * W, LANES), jnp.float32)
    gm[0:LANES, :] = em[0:LANES, :].T
    for b in range(per):
        stage2[pl.ds(b, T, stride=8), :] = gm[b * T : (b + 1) * T, :]
    begin(second)
    recv2[mine, :] = stage2[mine, :]
    finish(second)
    if per == 8:
        em[0:LANES, :] = recv2[...].T
    else:
        at_row = lax.broadcasted_iota(jnp.int32, (LANES, 8 * T), 0)
        at_col = lax.broadcasted_iota(jnp.int32, (LANES, 8 * T), 1)
        order = (at_col == (at_row // per) * 8 + at_row % per).astype(jnp.float32)
        em[0:LANES, :] = jnp.dot(
            order,
            recv2[...],
            precision=lax.Precision.HIGHEST,
            preferred_element_type=jnp.float32,
        ).T
    for o, ref in enumerate((fm_ref, sm_ref, sv_ref)):
        for i in range(W):
            ref[0:1, i * LANES : (i + 1) * LANES] = em[o * W + i : o * W + i + 1, :]


def body(T, observed, present, loading, noise_var, region_block, transition, innovation, pmean, pvar):
    regions = observed.shape[1]
    extra = -regions % CHUNK
    padded = regions + extra
    wide = ((0, 0), (0, extra))
    f32 = jnp.float32
    mat = pltpu.VMEM((W2, LANES), f32)
    vmem = pl.BlockSpec(memory_space=pltpu.VMEM)
    out = jax.ShapeDtypeStruct((1, W * LANES), f32)
    return pl.pallas_call(
        functools.partial(kernel, T),
        out_shape=(out, out, out),
        in_specs=[vmem] * 9,
        out_specs=(vmem, vmem, vmem),
        scratch_shapes=[
            pltpu.VMEM((LANES, 2 * LANES), f32),
            pltpu.VMEM((2, 8 * T, LANES), f32),
            pltpu.VMEM((2, 8 * T, LANES), f32),
            pltpu.VMEM((8 * T, LANES), f32),
            pltpu.VMEM((8 * T, LANES), f32),
            mat,
            mat,
            mat,
            mat,
            mat,
            mat,
            mat,
            mat,
            mat,
            pltpu.VMEM((W2 + 3 * W, LANES), f32),
            mat,
            pltpu.SemaphoreType.DMA((T,)),
            pltpu.SemaphoreType.DMA((T,)),
            pltpu.SemaphoreType.DMA((T,)),
            pltpu.SemaphoreType.DMA((T,)),
        ],
        compiler_params=pltpu.CompilerParams(
            collective_id=0, has_side_effects=True, vmem_limit_bytes=32 * 1024 * 1024
        ),
    )(
        jnp.pad(observed, wide),
        jnp.pad(present, wide),
        jnp.pad(loading.T, wide),
        jnp.pad(noise_var[None], wide, constant_values=1.0),
        jnp.pad(region_block[None], wide, constant_values=-1),
        transition.reshape(W2, LANES),
        innovation.reshape(W, LANES),
        pmean.reshape(W, LANES),
        pvar.reshape(W, LANES),
    )


def solution(mesh):
    T = mesh.shape["tm"]
    return jax.shard_map(
        functools.partial(body, T),
        mesh=mesh,
        in_specs=(
            P(("ens", "tm"), None),
            P(("ens", "tm"), None),
            P(),
            P(),
            P(),
            P(),
            P(),
            P(),
            P(),
        ),
        out_specs=(P(("ens", "tm"), None), P(("ens", "tm"), None), P(("ens", "tm"), None)),
        check_vma=False,
    )
```

```python
import functools
import jax
import jax.numpy as jnp
from jax import lax
from jax.experimental import pallas as pl
from jax.experimental.pallas import tpu as pltpu
from jax.sharding import PartitionSpec as P

MESH = pl.DeviceIdType.MESH
W = 16
W2 = W * W
LANES = 128
CHUNK = 512


def negative_inverse(rows):
    sub = lax.broadcasted_iota(jnp.int32, (W, LANES), 0)
    rows = list(rows)
    for p in range(W):
        row = rows[p]
        d = 1.0 / row[p : p + 1, :]
        here = sub == p
        scaled = jnp.where(here, -d, row * d)
        for i in range(W):
            if i == p:
                rows[i] = scaled
            else:
                rows[i] = jnp.where(here, 0.0, rows[i]) - row[i : i + 1, :] * scaled
    return rows


def store_rows(ref, rows):
    for i in range(W):
        ref[i * W : (i + 1) * W, :] = rows[i]


def load_rows(ref):
    return [ref[i * W : (i + 1) * W, :] for i in range(W)]


def load_columns(ref):
    return [ref[pl.ds(k, W, stride=W), :] for k in range(W)]


def multiply(out_ref, left_ref, right_rows, turned=False, start=None, mask=None):
    def one(i, carry):
        at = pl.multiple_of(i * W, W)
        total = None
        for k in range(W):
            row = k * W + i if turned else i * W + k
            term = left_ref[pl.ds(row, 1), :] * right_rows[k]
            total = term if total is None else total + term
        if start is not None:
            total = total + start[pl.ds(at, W), :]
        if mask is not None:
            total = jnp.where(mask, total, 0.0)
        out_ref[pl.ds(at, W), :] = total
        return carry

    lax.fori_loop(0, W, one, 0, unroll=4)


def weigh(rows, vector):
    total = rows[0] * vector[0:1, :]
    for k in range(1, W):
        total = total + rows[k] * vector[k : k + 1, :]
    return total


def kernel(
    T,
    obs_hbm,
    pres_hbm,
    load_hbm,
    nv_hbm,
    rb_hbm,
    trans_hbm,
    innov_hbm,
    pmean_hbm,
    pvar_hbm,
    fm_ref,
    sm_ref,
    sv_ref,
    obs_ref,
    pres_ref,
    load_ref,
    nv_ref,
    rb_ref,
    whole,
    fetch_sem,
    stage,
    recv,
    stage2,
    recv2,
    jm,
    km,
    ym,
    bm,
    nm,
    gm,
    em,
    j1,
    k1,
    const,
    info,
    send_sem,
    recv_sem,
    send_sem2,
    recv_sem2,
):
    per = LANES // T
    regions = obs_hbm.shape[1]
    me = lax.axis_index("tm")
    barrier = pltpu.get_barrier_semaphore()

    fetches = [
        pltpu.make_async_copy(src, dst, fetch_sem.at[n])
        for n, (src, dst) in enumerate(
            (
                (pres_hbm, pres_ref),
                (nv_hbm, nv_ref),
                (load_hbm, load_ref),
                (obs_hbm, obs_ref),
                (rb_hbm, rb_ref),
                (trans_hbm, whole.at[pl.ds(0, W2), :]),
                (innov_hbm, whole.at[pl.ds(W2, W), :]),
                (pmean_hbm, whole.at[pl.ds(W2 + W, W), :]),
                (pvar_hbm, whole.at[pl.ds(W2 + 2 * W, W), :]),
            )
        )
    ]
    for f in fetches:
        f.start()
    for k in range(1, T):
        pl.semaphore_signal(
            barrier, inc=1, device_id={"tm": lax.rem(me + k, T)}, device_id_type=MESH
        )
    for f in fetches[:5]:
        f.wait()

    row_at = lax.broadcasted_iota(jnp.int32, (LANES, 1), 0)
    block_of = (row_at % T) * per + row_at // T

    got = None
    for low_end in range(0, regions, CHUNK):
        wide = min(CHUNK, regions - low_end)
        at = slice(low_end, low_end + wide)
        weight = pres_ref[:, at].astype(jnp.float32) / nv_ref[:, at]
        load = load_ref[:, at]
        value = obs_ref[:, at]
        lw = load * weight
        parts = [lw * load]
        for d in range(1, W // 2 + 1):
            parts.append(lw * pltpu.roll(load, W - d, 0))
        parts.append(lw * value)
        high = [p.astype(jnp.bfloat16) for p in parts]
        low = [(p - h.astype(jnp.float32)).astype(jnp.bfloat16) for p, h in zip(parts, high)]
        fill = [jnp.zeros((2 * LANES - W * len(parts), wide), jnp.bfloat16)]
        onehot = (rb_ref[:, at] == block_of).astype(jnp.float32).astype(jnp.bfloat16)
        dims = (((1,), (1,)), ((), ()))
        new = lax.dot_general(
            onehot,
            jnp.concatenate(high + fill, axis=0),
            dims,
            preferred_element_type=jnp.float32,
        ) + lax.dot_general(
            onehot,
            jnp.concatenate(low + fill, axis=0),
            dims,
            preferred_element_type=jnp.float32,
        )

        got = new if got is None else got + new
    if per < 8:
        stage[...] = jnp.zeros_like(stage)
        stage2[...] = jnp.zeros_like(stage2)
    for h in range(2):
        for b in range(per):
            stage[h, pl.ds(b, T, stride=8), :] = got[
                b * T : (b + 1) * T, h * LANES : (h + 1) * LANES
            ]

    lane_from = lax.broadcasted_iota(jnp.int32, (LANES, LANES), 0)
    lane_to = lax.broadcasted_iota(jnp.int32, (LANES, LANES), 1)
    pick = (lane_from == me * per + lane_to // T).astype(jnp.float32)
    for f in fetches[5:]:
        f.wait()
    const[...] = jnp.dot(
        whole[...], pick, precision=lax.Precision.HIGHEST, preferred_element_type=jnp.float32
    )
    sub = lax.broadcasted_iota(jnp.int32, (W, LANES), 0)
    hour = lax.broadcasted_iota(jnp.int32, (W, LANES), 1) % T
    opening = hour == 0
    inv_noise = 1.0 / const[W2 : W2 + W, :]
    inv_prior = 1.0 / const[W2 + 2 * W : W2 + 3 * W, :]
    start_mean = const[W2 + W : W2 + 2 * W, :] * inv_prior
    for i in range(W):
        km[i * W : (i + 1) * W, :] = jnp.where(
            opening, 0.0, -const[i * W : (i + 1) * W, :] * inv_noise[i : i + 1, :]
        )
    flipped = [-r for r in load_rows(km)]
    multiply(jm, const, flipped, turned=True)
    bm[...] = jnp.zeros_like(bm)

    pl.semaphore_wait(barrier, T - 1)

    def first(k):
        peer = lax.rem(me + k, T)
        return pltpu.make_async_remote_copy(
            src_ref=stage.at[:, pl.ds(pl.multiple_of(peer * 8, 8), 8), :],
            dst_ref=recv.at[:, pl.ds(pl.multiple_of(me * 8, 8), 8), :],
            send_sem=send_sem,
            recv_sem=recv_sem,
            device_id={"tm": peer},
            device_id_type=MESH,
        )

    def second(k):
        peer = lax.rem(me + k, T)
        return pltpu.make_async_remote_copy(
            src_ref=stage2.at[pl.ds(pl.multiple_of(peer * 8, 8), 8), :],
            dst_ref=recv2.at[pl.ds(pl.multiple_of(me * 8, 8), 8), :],
            send_sem=send_sem2,
            recv_sem=recv_sem2,
            device_id={"tm": peer},
            device_id_type=MESH,
        )

    def begin(make):
        for k in range(1, T):
            make(k).start()

    begin(first)
    mine = pl.ds(pl.multiple_of(me * 8, 8), 8)
    recv[:, mine, :] = stage[:, mine, :]

    rest = pl.ds(0, (T - 1) * 8)
    pltpu.make_async_copy(recv.at[:, rest, :], recv.at[:, rest, :], recv_sem).wait()
    for h in range(2):
        joined = jnp.concatenate(
            [recv[h, pl.ds(b, T, stride=8), :] for b in range(per)], axis=0
        )
        info[h * LANES : (h + 1) * LANES, :] = joined.T
    diag = jnp.where(opening, inv_prior, inv_noise)
    for i in range(W):
        for j in range(W):
            gap = (j - i) % W
            row = gap * W + i if gap <= W // 2 else (W - gap) * W + j
            ym[i * W + j : i * W + j + 1, :] = info[row : row + 1, :]
    for i in range(W):
        ym[i * W : (i + 1) * W, :] += jnp.where(sub == i, diag, 0.0)
    npair = (W // 2 + 1) * W
    yv = info[npair : npair + W, :] + jnp.where(opening, start_mean, 0.0)
    ev = jnp.zeros((W, LANES), jnp.float32)
    bv = jnp.zeros((W, LANES), jnp.float32)

    rounds = (T - 1).bit_length()

    def doubling(step, carry):
        yv, ev, bv = carry
        s = jnp.left_shift(1, step)
        keep = hour + s <= T - 1
        rows = negative_inverse(
            [ym[i * W : (i + 1) * W, :] + bm[i * W : (i + 1) * W, :] for i in range(W)]
        )
        store_rows(nm, rows)
        drive = weigh(rows, yv + bv)
        krows = load_rows(km)
        xv = ev + weigh(krows, drive)
        multiply(gm, nm, krows)
        multiply(em, km, load_rows(gm), turned=True, start=jm)
        for i in range(W):
            at = slice(i * W, (i + 1) * W)
            bm[at, :] = jnp.where(keep, pltpu.roll(em[at, :], LANES - s, 1), bm[at, :])
        bv = jnp.where(keep, pltpu.roll(xv, LANES - s, 1), bv)
        inside = hour >= s
        for i in range(W):
            at = slice(i * W, (i + 1) * W)
            k1[at, :] = pltpu.roll(km[at, :], s, 1)
            j1[at, :] = pltpu.roll(jm[at, :], s, 1)
        rows = negative_inverse(
            [
                pltpu.roll(ym[i * W : (i + 1) * W, :], s, 1) + jm[i * W : (i + 1) * W, :]
                for i in range(W)
            ]
        )
        store_rows(nm, rows)
        drive = weigh(rows, pltpu.roll(yv, s, 1) + ev)
        columns = load_columns(km)
        yv = yv + weigh(columns, drive)
        multiply(em, nm, columns)
        multiply(ym, km, load_rows(em), start=ym)
        k1rows = load_rows(k1)
        ev = jnp.where(inside, pltpu.roll(ev, s, 1) + weigh(k1rows, drive), 0.0)
        multiply(gm, nm, k1rows)
        grows = load_rows(gm)
        multiply(jm, k1, grows, turned=True, start=j1, mask=inside)
        multiply(em, km, grows)
        km[...] = em[...]
        return yv, ev, bv

    yv, ev, bv = lax.fori_loop(0, rounds, doubling, (yv, ev, bv))

    rows = negative_inverse(load_rows(ym))
    em[0:W, :] = -weigh(rows, yv)
    rows = negative_inverse(
        [ym[i * W : (i + 1) * W, :] + bm[i * W : (i + 1) * W, :] for i in range(W)]
    )
    em[W : 2 * W, :] = -weigh(rows, yv + bv)
    spread = jnp.where(sub == 0, rows[0], 0.0)
    for i in range(1, W):
        spread = spread + jnp.where(sub == i, rows[i], 0.0)
    em[2 * W : 3 * W, :] = -spread
    em[3 * W : 8 * W, :] = jnp.zeros((5 * W, LANES), jnp.float32)
    gm[0:LANES, :] = em[0:LANES, :].T
    for b in range(per):
        stage2[pl.ds(b, T, stride=8), :] = gm[b * T : (b + 1) * T, :]
    begin(second)
    recv2[mine, :] = stage2[mine, :]
    pltpu.make_async_copy(recv2.at[rest, :], recv2.at[rest, :], recv_sem2).wait()
    if per == 8:
        em[0:LANES, :] = recv2[...].T
    else:
        at_row = lax.broadcasted_iota(jnp.int32, (LANES, 8 * T), 0)
        at_col = lax.broadcasted_iota(jnp.int32, (LANES, 8 * T), 1)
        order = (at_col == (at_row // per) * 8 + at_row % per).astype(jnp.float32)
        em[0:LANES, :] = jnp.dot(
            order,
            recv2[...],
            precision=lax.Precision.HIGHEST,
            preferred_element_type=jnp.float32,
        ).T
    for o, ref in enumerate((fm_ref, sm_ref, sv_ref)):
        for i in range(W):
            ref[0:1, i * LANES : (i + 1) * LANES] = em[o * W + i : o * W + i + 1, :]
    pltpu.make_async_copy(stage.at[:, rest, :], stage.at[:, rest, :], send_sem).wait()
    pltpu.make_async_copy(stage2.at[rest, :], stage2.at[rest, :], send_sem2).wait()


def body(T, observed, present, loading, noise_var, region_block, transition, innovation, pmean, pvar):
    regions = observed.shape[1]
    f32 = jnp.float32
    mat = pltpu.VMEM((W2, LANES), f32)
    vmem = pl.BlockSpec(memory_space=pltpu.VMEM)
    out = jax.ShapeDtypeStruct((1, W * LANES), f32)
    return pl.pallas_call(
        functools.partial(kernel, T),
        out_shape=(out, out, out),
        in_specs=[pl.BlockSpec(memory_space=pl.ANY)] * 9,
        out_specs=(vmem, vmem, vmem),
        scratch_shapes=[
            pltpu.VMEM((1, regions), f32),
            pltpu.VMEM((1, regions), jnp.int32),
            pltpu.VMEM((W, regions), f32),
            pltpu.VMEM((1, regions), f32),
            pltpu.VMEM((1, regions), jnp.int32),
            pltpu.VMEM((W2 + 3 * W, LANES), f32),
            pltpu.SemaphoreType.DMA((9,)),
            pltpu.VMEM((2, 8 * T, LANES), f32),
            pltpu.VMEM((2, 8 * T, LANES), f32),
            pltpu.VMEM((8 * T, LANES), f32),
            pltpu.VMEM((8 * T, LANES), f32),
            mat,
            mat,
            mat,
            mat,
            mat,
            mat,
            mat,
            mat,
            mat,
            pltpu.VMEM((W2 + 3 * W, LANES), f32),
            mat,
            pltpu.SemaphoreType.DMA,
            pltpu.SemaphoreType.DMA,
            pltpu.SemaphoreType.DMA,
            pltpu.SemaphoreType.DMA,
        ],
        compiler_params=pltpu.CompilerParams(
            collective_id=0, has_side_effects=True, vmem_limit_bytes=32 * 1024 * 1024
        ),
    )(
        observed,
        present,
        loading.T,
        noise_var[None],
        region_block[None],
        transition.reshape(W2, LANES),
        innovation.reshape(W, LANES),
        pmean.reshape(W, LANES),
        pvar.reshape(W, LANES),
    )


def solution(mesh):
    T = mesh.shape["tm"]
    return jax.shard_map(
        functools.partial(body, T),
        mesh=mesh,
        in_specs=(
            P(("ens", "tm"), None),
            P(("ens", "tm"), None),
            P(),
            P(),
            P(),
            P(),
            P(),
            P(),
            P(),
        ),
        out_specs=(P(("ens", "tm"), None), P(("ens", "tm"), None), P(("ens", "tm"), None)),
        check_vma=False,
    )
```

```python
import functools
import jax
import jax.numpy as jnp
from jax import lax
from jax.experimental import pallas as pl
from jax.experimental.pallas import tpu as pltpu
from jax.sharding import PartitionSpec as P

MESH = pl.DeviceIdType.MESH
W = 16
W2 = W * W
LANES = 128
CHUNK = 512


def negative_inverse(rows):
    sub = lax.broadcasted_iota(jnp.int32, (W, LANES), 0)
    rows = list(rows)
    for p in range(W):
        row = rows[p]
        d = 1.0 / row[p : p + 1, :]
        here = sub == p
        scaled = jnp.where(here, -d, row * d)
        for i in range(W):
            if i == p:
                rows[i] = scaled
            else:
                rows[i] = jnp.where(here, 0.0, rows[i]) - row[i : i + 1, :] * scaled
    return rows


def store_rows(ref, rows):
    for i in range(W):
        ref[i * W : (i + 1) * W, :] = rows[i]


def load_rows(ref):
    return [ref[i * W : (i + 1) * W, :] for i in range(W)]


def load_columns(ref):
    return [ref[pl.ds(k, W, stride=W), :] for k in range(W)]


def multiply(out_ref, left_ref, right_rows, turned=False, start=None, mask=None):
    def one(i, carry):
        at = pl.multiple_of(i * W, W)
        total = None
        for k in range(W):
            row = k * W + i if turned else i * W + k
            term = left_ref[pl.ds(row, 1), :] * right_rows[k]
            total = term if total is None else total + term
        if start is not None:
            total = total + start[pl.ds(at, W), :]
        if mask is not None:
            total = jnp.where(mask, total, 0.0)
        out_ref[pl.ds(at, W), :] = total
        return carry

    lax.fori_loop(0, W, one, 0, unroll=4)


def weigh(rows, vector):
    total = rows[0] * vector[0:1, :]
    for k in range(1, W):
        total = total + rows[k] * vector[k : k + 1, :]
    return total


def kernel(
    T,
    obs_hbm,
    pres_hbm,
    load_hbm,
    nv_hbm,
    rb_hbm,
    trans_hbm,
    innov_hbm,
    pmean_hbm,
    pvar_hbm,
    out_ref,
    obs_ref,
    pres_ref,
    load_ref,
    nv_ref,
    rb_ref,
    whole,
    fetch_sem,
    stage,
    recv,
    stage2,
    recv2,
    jm,
    km,
    ym,
    bm,
    nm,
    gm,
    em,
    j1,
    k1,
    const,
    info,
    send_sem,
    recv_sem,
    send_sem2,
    recv_sem2,
):
    per = LANES // T
    regions = obs_hbm.shape[1]
    me = lax.axis_index("tm")
    barrier = pltpu.get_barrier_semaphore()

    fetches = [
        pltpu.make_async_copy(src, dst, fetch_sem.at[n])
        for n, (src, dst) in enumerate(
            (
                (pres_hbm, pres_ref),
                (nv_hbm, nv_ref),
                (load_hbm, load_ref),
                (obs_hbm, obs_ref),
                (rb_hbm, rb_ref),
                (trans_hbm, whole.at[pl.ds(0, W2), :]),
                (innov_hbm, whole.at[pl.ds(W2, W), :]),
                (pmean_hbm, whole.at[pl.ds(W2 + W, W), :]),
                (pvar_hbm, whole.at[pl.ds(W2 + 2 * W, W), :]),
            )
        )
    ]
    for f in fetches:
        f.start()
    for k in range(1, T):
        pl.semaphore_signal(
            barrier, inc=1, device_id={"tm": lax.rem(me + k, T)}, device_id_type=MESH
        )
    for f in fetches[:5]:
        f.wait()

    row_at = lax.broadcasted_iota(jnp.int32, (LANES, 1), 0)
    block_of = (row_at % T) * per + row_at // T

    got = None
    for low_end in range(0, regions, CHUNK):
        wide = min(CHUNK, regions - low_end)
        at = slice(low_end, low_end + wide)
        weight = pres_ref[:, at].astype(jnp.float32) / nv_ref[:, at]
        load = load_ref[:, at]
        value = obs_ref[:, at]
        lw = load * weight
        parts = [lw * load]
        for d in range(1, W // 2 + 1):
            parts.append(lw * pltpu.roll(load, W - d, 0))
        parts.append(lw * value)
        high = [p.astype(jnp.bfloat16) for p in parts]
        low = [(p - h.astype(jnp.float32)).astype(jnp.bfloat16) for p, h in zip(parts, high)]
        fill = [jnp.zeros((2 * LANES - W * len(parts), wide), jnp.bfloat16)]
        onehot = (rb_ref[:, at] == block_of).astype(jnp.float32).astype(jnp.bfloat16)
        dims = (((1,), (1,)), ((), ()))
        new = lax.dot_general(
            onehot,
            jnp.concatenate(high + fill, axis=0),
            dims,
            preferred_element_type=jnp.float32,
        ) + lax.dot_general(
            onehot,
            jnp.concatenate(low + fill, axis=0),
            dims,
            preferred_element_type=jnp.float32,
        )

        got = new if got is None else got + new
    if per < 8:
        stage[...] = jnp.zeros_like(stage)
        stage2[...] = jnp.zeros_like(stage2)
    for h in range(2):
        for b in range(per):
            stage[h, pl.ds(b, T, stride=8), :] = got[
                b * T : (b + 1) * T, h * LANES : (h + 1) * LANES
            ]

    lane_from = lax.broadcasted_iota(jnp.int32, (LANES, LANES), 0)
    lane_to = lax.broadcasted_iota(jnp.int32, (LANES, LANES), 1)
    pick = (lane_from == me * per + lane_to // T).astype(jnp.float32)
    for f in fetches[5:]:
        f.wait()
    const[...] = jnp.dot(
        whole[...], pick, precision=lax.Precision.HIGHEST, preferred_element_type=jnp.float32
    )
    sub = lax.broadcasted_iota(jnp.int32, (W, LANES), 0)
    hour = lax.broadcasted_iota(jnp.int32, (W, LANES), 1) % T
    opening = hour == 0
    inv_noise = 1.0 / const[W2 : W2 + W, :]
    inv_prior = 1.0 / const[W2 + 2 * W : W2 + 3 * W, :]
    start_mean = const[W2 + W : W2 + 2 * W, :] * inv_prior
    for i in range(W):
        km[i * W : (i + 1) * W, :] = jnp.where(
            opening, 0.0, -const[i * W : (i + 1) * W, :] * inv_noise[i : i + 1, :]
        )
    flipped = [-r for r in load_rows(km)]
    multiply(jm, const, flipped, turned=True)
    bm[...] = jnp.zeros_like(bm)

    pl.semaphore_wait(barrier, T - 1)

    def first(k):
        peer = lax.rem(me + k, T)
        return pltpu.make_async_remote_copy(
            src_ref=stage.at[:, pl.ds(pl.multiple_of(peer * 8, 8), 8), :],
            dst_ref=recv.at[:, pl.ds(pl.multiple_of(me * 8, 8), 8), :],
            send_sem=send_sem,
            recv_sem=recv_sem,
            device_id={"tm": peer},
            device_id_type=MESH,
        )

    def second(k):
        peer = lax.rem(me + k, T)
        return pltpu.make_async_remote_copy(
            src_ref=stage2.at[pl.ds(pl.multiple_of(peer * 8, 8), 8), :],
            dst_ref=recv2.at[pl.ds(pl.multiple_of(me * 8, 8), 8), :],
            send_sem=send_sem2,
            recv_sem=recv_sem2,
            device_id={"tm": peer},
            device_id_type=MESH,
        )

    def begin(make):
        for k in range(1, T):
            make(k).start()

    begin(first)
    mine = pl.ds(pl.multiple_of(me * 8, 8), 8)
    recv[:, mine, :] = stage[:, mine, :]

    rest = pl.ds(0, (T - 1) * 8)
    pltpu.make_async_copy(recv.at[:, rest, :], recv.at[:, rest, :], recv_sem).wait()
    for h in range(2):
        joined = jnp.concatenate(
            [recv[h, pl.ds(b, T, stride=8), :] for b in range(per)], axis=0
        )
        info[h * LANES : (h + 1) * LANES, :] = joined.T
    diag = jnp.where(opening, inv_prior, inv_noise)
    for i in range(W):
        for j in range(W):
            gap = (j - i) % W
            row = gap * W + i if gap <= W // 2 else (W - gap) * W + j
            ym[i * W + j : i * W + j + 1, :] = info[row : row + 1, :]
    for i in range(W):
        ym[i * W : (i + 1) * W, :] += jnp.where(sub == i, diag, 0.0)
    npair = (W // 2 + 1) * W
    yv = info[npair : npair + W, :] + jnp.where(opening, start_mean, 0.0)
    ev = jnp.zeros((W, LANES), jnp.float32)
    bv = jnp.zeros((W, LANES), jnp.float32)

    rounds = (T - 1).bit_length()

    def doubling(step, carry):
        yv, ev, bv = carry
        s = jnp.left_shift(1, step)
        keep = hour + s <= T - 1
        rows = negative_inverse(
            [ym[i * W : (i + 1) * W, :] + bm[i * W : (i + 1) * W, :] for i in range(W)]
        )
        store_rows(nm, rows)
        drive = weigh(rows, yv + bv)
        krows = load_rows(km)
        xv = ev + weigh(krows, drive)
        multiply(gm, nm, krows)
        multiply(em, km, load_rows(gm), turned=True, start=jm)
        for i in range(W):
            at = slice(i * W, (i + 1) * W)
            bm[at, :] = jnp.where(keep, pltpu.roll(em[at, :], LANES - s, 1), bm[at, :])
        bv = jnp.where(keep, pltpu.roll(xv, LANES - s, 1), bv)
        inside = hour >= s
        for i in range(W):
            at = slice(i * W, (i + 1) * W)
            k1[at, :] = pltpu.roll(km[at, :], s, 1)
            j1[at, :] = pltpu.roll(jm[at, :], s, 1)
        rows = negative_inverse(
            [
                pltpu.roll(ym[i * W : (i + 1) * W, :], s, 1) + jm[i * W : (i + 1) * W, :]
                for i in range(W)
            ]
        )
        store_rows(nm, rows)
        drive = weigh(rows, pltpu.roll(yv, s, 1) + ev)
        columns = load_columns(km)
        yv = yv + weigh(columns, drive)
        multiply(em, nm, columns)
        multiply(ym, km, load_rows(em), start=ym)
        k1rows = load_rows(k1)
        ev = jnp.where(inside, pltpu.roll(ev, s, 1) + weigh(k1rows, drive), 0.0)
        multiply(gm, nm, k1rows)
        grows = load_rows(gm)
        multiply(jm, k1, grows, turned=True, start=j1, mask=inside)
        multiply(em, km, grows)
        km[...] = em[...]
        return yv, ev, bv

    yv, ev, bv = lax.fori_loop(0, rounds, doubling, (yv, ev, bv))

    rows = negative_inverse(load_rows(ym))
    em[0:W, :] = -weigh(rows, yv)
    rows = negative_inverse(
        [ym[i * W : (i + 1) * W, :] + bm[i * W : (i + 1) * W, :] for i in range(W)]
    )
    em[W : 2 * W, :] = -weigh(rows, yv + bv)
    spread = jnp.where(sub == 0, rows[0], 0.0)
    for i in range(1, W):
        spread = spread + jnp.where(sub == i, rows[i], 0.0)
    em[2 * W : 3 * W, :] = -spread
    em[3 * W : 8 * W, :] = jnp.zeros((5 * W, LANES), jnp.float32)
    gm[0:LANES, :] = em[0:LANES, :].T
    for b in range(per):
        stage2[pl.ds(b, T, stride=8), :] = gm[b * T : (b + 1) * T, :]
    begin(second)
    recv2[mine, :] = stage2[mine, :]
    pltpu.make_async_copy(recv2.at[rest, :], recv2.at[rest, :], recv_sem2).wait()
    out_ref[...] = recv2[...]
    pltpu.make_async_copy(stage.at[:, rest, :], stage.at[:, rest, :], send_sem).wait()
    pltpu.make_async_copy(stage2.at[rest, :], stage2.at[rest, :], send_sem2).wait()


def arrange(T, got_ref, fm_ref, sm_ref, sv_ref):
    per = LANES // T
    if per == 8:
        full = got_ref[...].T
    else:
        at_row = lax.broadcasted_iota(jnp.int32, (LANES, 8 * T), 0)
        at_col = lax.broadcasted_iota(jnp.int32, (LANES, 8 * T), 1)
        order = (at_col == (at_row // per) * 8 + at_row % per).astype(jnp.float32)
        full = jnp.dot(
            order,
            got_ref[...],
            precision=lax.Precision.HIGHEST,
            preferred_element_type=jnp.float32,
        ).T
    for o, ref in enumerate((fm_ref, sm_ref, sv_ref)):
        for i in range(W):
            ref[0:1, i * LANES : (i + 1) * LANES] = full[o * W + i : o * W + i + 1, :]


def body(T, observed, present, loading, noise_var, region_block, transition, innovation, pmean, pvar):
    regions = observed.shape[1]
    f32 = jnp.float32
    mat = pltpu.VMEM((W2, LANES), f32)
    vmem = pl.BlockSpec(memory_space=pltpu.VMEM)
    out = jax.ShapeDtypeStruct((1, W * LANES), f32)
    got = pl.pallas_call(
        functools.partial(kernel, T),
        out_shape=jax.ShapeDtypeStruct((8 * T, LANES), f32),
        in_specs=[pl.BlockSpec(memory_space=pl.ANY)] * 9,
        out_specs=vmem,
        scratch_shapes=[
            pltpu.VMEM((1, regions), f32),
            pltpu.VMEM((1, regions), jnp.int32),
            pltpu.VMEM((W, regions), f32),
            pltpu.VMEM((1, regions), f32),
            pltpu.VMEM((1, regions), jnp.int32),
            pltpu.VMEM((W2 + 3 * W, LANES), f32),
            pltpu.SemaphoreType.DMA((9,)),
            pltpu.VMEM((2, 8 * T, LANES), f32),
            pltpu.VMEM((2, 8 * T, LANES), f32),
            pltpu.VMEM((8 * T, LANES), f32),
            pltpu.VMEM((8 * T, LANES), f32),
            mat,
            mat,
            mat,
            mat,
            mat,
            mat,
            mat,
            mat,
            mat,
            pltpu.VMEM((W2 + 3 * W, LANES), f32),
            mat,
            pltpu.SemaphoreType.DMA,
            pltpu.SemaphoreType.DMA,
            pltpu.SemaphoreType.DMA,
            pltpu.SemaphoreType.DMA,
        ],
        compiler_params=pltpu.CompilerParams(
            collective_id=0, has_side_effects=True, vmem_limit_bytes=63 * 1024 * 1024
        ),
    )(
        observed,
        present,
        loading.T,
        noise_var[None],
        region_block[None],
        transition.reshape(W2, LANES),
        innovation.reshape(W, LANES),
        pmean.reshape(W, LANES),
        pvar.reshape(W, LANES),
    )
    return pl.pallas_call(
        functools.partial(arrange, T),
        out_shape=(out, out, out),
        in_specs=[vmem],
        out_specs=(vmem, vmem, vmem),
    )(got)


def solution(mesh):
    T = mesh.shape["tm"]
    return jax.shard_map(
        functools.partial(body, T),
        mesh=mesh,
        in_specs=(
            P(("ens", "tm"), None),
            P(("ens", "tm"), None),
            P(),
            P(),
            P(),
            P(),
            P(),
            P(),
            P(),
        ),
        out_specs=(P(("ens", "tm"), None), P(("ens", "tm"), None), P(("ens", "tm"), None)),
        check_vma=False,
    )
```
